32 devices in a mesh: groups: 2 (over x), space: 8 (over z, y), dp: 2 (over core).
Axes of the slice: x: 2, y: 2, z: 4, core: 2. Of those that a mesh axis runs over, the one named last changes fastest.
Arguments:
- features: bfloat16 [4, 3072, 256], P(('groups', 'dp'), 'space'), parts along dimension 0, may hold values from -6 to 6
- positions: float32 [4, 3, 3072], P(('groups', 'dp'), None, 'space'), parts along dimension 0, may hold values from 0 to 3
- species: int32 [4, 3072], P(('groups', 'dp'), 'space'), parts along dimension 0, may hold values from 0 to 9
- ghost_ids: int32 [4, 8, 128], P(('groups', 'dp'), 'space'), parts along dimension 0, may hold values from -1 to 3071, as said below
- tile_mask: int32 [4, 8, 6, 8], P(('groups', 'dp'), 'space'), parts along dimension 0, may hold values from 0 to 1, as said below
- energy_grad: float32 [4, 3072], P(('groups', 'dp'), 'space'), parts along dimension 0, may hold values from -12 to 12
- w_proj: bfloat16 [256, 256], replicated, may hold values from -0.375 to 0.375
- w_radial: float32 [4, 256], replicated, may hold values from -3 to 3
- w_mix: float32 [4, 256], replicated, may hold values from -3 to 3
- w_update: bfloat16 [256, 256], replicated, may hold values from -0.375 to 0.375
- w_out: bfloat16 [256], replicated, may hold values from -0.375 to 0.375
- skip_gain: float32 [10, 256], replicated, may hold values from 0.1 to 1.9
Outputs:
- energies: float32 [4, 3072], P(('groups', 'dp'), 'space'), parts along dimension 0
- feature_grad: float32 [4, 3072, 256], P(('groups', 'dp'), 'space'), parts along dimension 0
- proj_grad: float32 [512, 256], P('groups'), parts along dimension 0
- radial_grad: float32 [8, 256], P('groups'), parts along dimension 0
- mix_grad: float32 [8, 256], P('groups'), parts along dimension 0
- update_grad: float32 [512, 256], P('groups'), parts along dimension 0
- out_grad: float32 [512], P('groups'), parts along dimension 0
- skip_grad: float32 [20, 256], P('groups'), parts along dimension 0
The draws below stay inside these ranges and needn't reach their ends.
There are 2 independent parts, one for each index of `groups`. The reference program is written for one: setup_inputs(seed, part) draws one part's arguments, and reference() takes and returns one part's arrays. A program takes and returns all parts, laid end to end along the dimension named above; an argument that names none is the same for every part. Nothing has to cross between parts.
Inputs may be any that keep to these rules, and one draw needn't show every extreme that they name: `ghost_ids`: slot s of domain d holds -1 (an empty slot) or the index of an atom owned by domain d - 1 or d + 1. Live slots come before empty ones, and in every configuration some domain has all 128 slots live. `tile_mask`: 1 where the 64 owned atoms of a tile interact with the 64 near rows of another tile.
All inputs are finite; a program needn't handle non-finite values.
Results may differ from the reference program's by a relative error of at most 0.012.
The reference program's roundings to bfloat16 on the way count: a program that leaves them out, or rounds other values in their place, can miss the bound.
Values may be sent and summed in bfloat16 or wider, within the bound.
A program may use at most 64 MiB of HBM per device.

```python
import math
import jax
import jax.numpy as jnp
import numpy as np
from jax import lax

C = 256
RADIAL = 4
SPECIES = 10
ATOM_DEV = 384
GHOST = 128
TILES_OWN = 6
TILES_NEAR = 8
CONFIGS = 2
ATOMS = 3072
N_SPACE = 8


def draw_ghost_ids(key, part):
    key = jax.random.fold_in(key, 11)
    side_key, row_key, count_key, full_key = jax.random.split(key, 4)
    grid_shape = (CONFIGS, N_SPACE, GHOST)
    domain_index = jnp.arange(N_SPACE, dtype=jnp.int32)[None, :, None]
    side_pick = jax.random.randint(side_key, grid_shape, 0, 2)
    side_pick = jnp.where(domain_index == 0, 1, jnp.where(domain_index == N_SPACE - 1, 0, side_pick))
    row_pick = jax.random.randint(row_key, grid_shape, 0, ATOM_DEV)
    slot_index = jnp.arange(GHOST, dtype=jnp.int32)[None, None, :]
    forced = (domain_index == N_SPACE - 2) & (slot_index == 0)
    side_pick = jnp.where(forced, 1, side_pick)
    row_pick = jnp.where(forced, ATOM_DEV - 1, row_pick)
    atom_index = jnp.where(side_pick == 0, (domain_index - 1) * ATOM_DEV + row_pick, (domain_index + 1) * ATOM_DEV + row_pick)
    live_count = jax.random.randint(count_key, (CONFIGS, N_SPACE, 1), GHOST // 4, GHOST)
    full_domain = jax.random.randint(full_key, (CONFIGS, 1, 1), 1, N_SPACE)
    live_count = jnp.where(domain_index == full_domain, GHOST, live_count)
    return jnp.where(slot_index < live_count, atom_index, -1).astype(jnp.int32)


def draw_tile_mask(key, part):
    key = jax.random.fold_in(key, 12)
    level_key, tile_key = jax.random.split(key)
    density = jax.random.randint(level_key, (CONFIGS, N_SPACE, 1, 1), 1, 5)
    raw_draw = jax.random.randint(tile_key, (CONFIGS, N_SPACE, TILES_OWN, TILES_NEAR), 0, 4)
    return (raw_draw < density).astype(jnp.int32)


def draw_energy_grad(key, part):
    key = jax.random.fold_in(key, 13)
    domain_index = jnp.arange(ATOMS, dtype=jnp.int32) // ATOM_DEV
    ramp = 1.0 + 2.0 * domain_index.astype(jnp.float32) / (N_SPACE - 1)
    base_value = jnp.clip(jax.random.normal(key, (CONFIGS, ATOMS), jnp.float32), -4.0, 4.0)
    return base_value * ramp[None, :]


def with_ends(values, stream_key, smallest, top_value):
    extent = values.shape
    index_at = [jax.random.randint(jax.random.fold_in(stream_key, axis), (), 0, extent[axis]) for axis in range(len(extent))]
    values = values.at[tuple(index_at)].set(smallest)
    longest = extent.index(max(extent))
    index_at[longest] = (index_at[longest] + 1) % extent[longest]
    return values.at[tuple(index_at)].set(top_value)


def block_levels(own_key, extent, cuts, smallest, high):
    level, own = 1.0, jax.random.fold_in(own_key, 6)
    for axis_at, parts in cuts:
        steps = jnp.exp(jax.random.uniform(jax.random.fold_in(own, axis_at), (parts,), jnp.float32, smallest / len(cuts), high / len(cuts)))
        level = level * jnp.repeat(steps, extent[axis_at] // parts).reshape([-1 if axis == axis_at else 1 for axis in range(len(extent))])
    return level


def rank_bounds(number_of, skew):
    portions = [(1 << 20) // math.isqrt(rank ** skew) + 1 for rank in range(1, number_of + 1)]
    scale = 1 + sum(portions) // (1 << 30)
    return np.cumsum(np.array([max(1, weight // scale) for weight in portions]))


def ranked(own_key, extent, number_of, lean):
    table = rank_bounds(number_of, lean)
    pick = jax.random.randint(jax.random.fold_in(own_key, 1), extent, 0, int(table[number_of - 1]))
    rank = jnp.searchsorted(jnp.asarray(table, jnp.int32), pick, side="right")
    return jax.random.permutation(jax.random.fold_in(own_key, 2), number_of)[rank].astype(jnp.int32)


def centred(rng, shape, scale, limit, shards=(), kind=jnp.bfloat16):
    result = scale * jax.random.normal(rng, shape, jnp.float32)
    if shards:
        result = result * block_levels(rng, shape, shards, -0.22, 0.18)
    return jnp.clip(result, -limit, limit).astype(kind)


def setup_inputs(seed: int = 0, part: int = 0) -> dict:
    key_list = jax.random.split(jax.random.key(seed), 13)
    part_splits = jax.random.split(jax.random.fold_in(key_list[12], part), 13)
    return {
        "features": centred(part_splits[0], (CONFIGS, ATOMS, C), 1.0, 6.0, ((0, 2), (1, 8))),
        "positions": jnp.clip(3.0 * jax.random.uniform(part_splits[1], (CONFIGS, 3, ATOMS), jnp.float32) ** block_levels(part_splits[1], (CONFIGS, 3, ATOMS), ((0, 2), (2, 8)), -0.2, 0.2), 0.0, 3.0),
        "species": with_ends(ranked(part_splits[2], (CONFIGS, ATOMS), SPECIES, 2), jax.random.fold_in(part_splits[2], 3), 0, SPECIES - 1).astype(jnp.int32),
        "ghost_ids": draw_ghost_ids(jax.random.fold_in(jax.random.fold_in(key_list[12], part), 71), part),
        "tile_mask": draw_tile_mask(jax.random.fold_in(jax.random.fold_in(key_list[12], part), 71), part),
        "energy_grad": draw_energy_grad(jax.random.fold_in(jax.random.fold_in(key_list[12], part), 71), part),
        "w_proj": centred(key_list[6], (C, C), C ** -0.5, 0.375),
        "w_radial": centred(key_list[7], (RADIAL, C), RADIAL ** -0.5, 3.0, (), jnp.float32),
        "w_mix": centred(key_list[8], (4, C), 0.5, 3.0, (), jnp.float32),
        "w_update": centred(key_list[9], (C, C), C ** -0.5, 0.375),
        "w_out": centred(key_list[10], (C,), C ** -0.5, 0.375),
        "skip_gain": jnp.clip(1.0 + 0.18 * jax.random.normal(key_list[11], (SPECIES, C), jnp.float32), 0.1, 1.9),
    }


neighbour_scale = 0.0625
radial_step = 0.8

def edge_terms(own_pos, near_pos, pair_mask, radial_count):
    delta_x = near_pos[0][None, :] - own_pos[0][:, None]
    delta_y = near_pos[1][None, :] - own_pos[1][:, None]
    delta_z = near_pos[2][None, :] - own_pos[2][:, None]
    distance = jnp.sqrt(delta_x * delta_x + delta_y * delta_y + delta_z * delta_z)
    root_three = math.sqrt(3.0)
    shapes = jnp.stack([jnp.ones_like(delta_x), delta_x, delta_y, delta_z, root_three * delta_x * delta_y, root_three * delta_y * delta_z, 0.5 * (2.0 * delta_z * delta_z - delta_x * delta_x - delta_y * delta_y), root_three * delta_x * delta_z, 0.5 * root_three * (delta_x * delta_x - delta_y * delta_y)])
    centres = radial_step * jnp.arange(radial_count).astype(jnp.float32)
    radial = jnp.exp(-jnp.square(distance[None] - centres[:, None, None]))
    weighted = shapes[:, None] * radial[None] * pair_mask[None, None]
    return weighted.reshape(9 * radial_count, delta_x.shape[0], delta_x.shape[1]).astype(jnp.bfloat16)

def pair_weights(tile_block, row_count, near_count):
    tile_size = row_count // tile_block.shape[0]
    spread = jnp.repeat(jnp.repeat(tile_block, tile_size, axis=0), tile_size, axis=1).astype(jnp.float32)
    apart = (jnp.arange(row_count, dtype=jnp.int32)[:, None] != jnp.arange(near_count, dtype=jnp.int32)[None, :]).astype(jnp.float32)
    return spread * apart

def rows_pass(own_h, own_pos, pair_mask, species_ids, energy_cot, near_x, near_pos, w_radial, w_mix, w_update, w_out, skip_gain):
    radial_count, channels = w_radial.shape
    row_count = own_h.shape[0]
    precise = lax.Precision.HIGHEST
    edge_table = edge_terms(own_pos, near_pos, pair_mask, radial_count)
    moments = jnp.dot(edge_table.reshape(-1, near_x.shape[0]), near_x, preferred_element_type=jnp.float32)
    moments = moments.reshape(9, radial_count, row_count, channels) * neighbour_scale
    density = lax.optimization_barrier(jnp.sum(w_radial[None, :, None, :] * moments, axis=1))
    invariants = jnp.stack([density[0], density[0] * density[0], lax.optimization_barrier(jnp.sum(density[1:4] * density[1:4], axis=0)), lax.optimization_barrier(jnp.sum(density[4:9] * density[4:9], axis=0))])
    mixed = lax.optimization_barrier(jnp.sum(w_mix[:, None, :] * invariants, axis=0)).astype(jnp.bfloat16)
    species_hot = (species_ids[:, None] == jnp.arange(skip_gain.shape[0], dtype=jnp.int32)[None, :]).astype(jnp.float32)
    skip_row = jnp.dot(species_hot, skip_gain, precision=precise)
    own_float = own_h.astype(jnp.float32)
    update = jnp.dot(mixed, w_update, preferred_element_type=jnp.float32) + own_float * skip_row
    readout = w_out.astype(jnp.float32)
    active = jax.nn.silu(update)
    energy = lax.optimization_barrier(jnp.sum(active * readout[None, :], axis=1))
    logistic = jax.nn.sigmoid(update)
    update_cot = energy_cot[:, None] * readout[None, :] * (logistic * (1.0 + update * (1.0 - logistic)))
    cot_bf = update_cot.astype(jnp.bfloat16)
    mixed_cot = lax.dot_general(cot_bf, w_update, (((1,), (1,)), ((), ())), preferred_element_type=jnp.float32)
    d_update = lax.dot_general(mixed, cot_bf, (((0,), (0,)), ((), ())), preferred_element_type=jnp.float32)
    d_mix = lax.optimization_barrier(jnp.sum(mixed_cot[None] * invariants, axis=1))
    d_out = lax.optimization_barrier(jnp.sum(energy_cot[:, None] * active, axis=0))
    d_skip = lax.dot_general(species_hot, update_cot * own_float, (((0,), (0,)), ((), ())), precision=precise)
    weighted = w_mix[:, None, :] * mixed_cot[None]
    leading = weighted[0] + 2.0 * weighted[1] * density[0]
    density_cot = jnp.concatenate([leading[None], 2.0 * weighted[2][None] * density[1:4], 2.0 * weighted[3][None] * density[4:9]], axis=0)
    d_radial = lax.optimization_barrier(jnp.sum(density_cot[:, None] * moments, axis=(0, 2)))
    moment_cot = (density_cot[:, None] * w_radial[None, :, None, :]).astype(jnp.bfloat16)
    return (edge_table, moment_cot, energy, update_cot * skip_row, (d_update, d_mix, d_radial, d_out, d_skip))

def reference(features, positions, species, ghost_ids, tile_mask, energy_grad, w_proj, w_radial, w_mix, w_update, w_out, skip_gain):
    domain_count = CONFIGS * N_SPACE
    near_count = ATOM_DEV + GHOST
    projected = jnp.dot(features.reshape(-1, C), w_proj, preferred_element_type=jnp.float32)
    projected = projected.astype(jnp.bfloat16).reshape(CONFIGS, ATOMS, C)
    is_live = (ghost_ids >= 0).reshape(CONFIGS, N_SPACE * GHOST)
    safe_ids = jnp.where(is_live, ghost_ids.reshape(CONFIGS, N_SPACE * GHOST), 0).astype(jnp.int32)
    ghost_rows = jnp.take_along_axis(projected, safe_ids[:, :, None], axis=1)
    ghost_rows = jnp.where(is_live[:, :, None], ghost_rows, jnp.zeros_like(ghost_rows))
    place_ids = jnp.broadcast_to(safe_ids[:, None, :], (CONFIGS, 3, N_SPACE * GHOST))
    ghost_pos = jnp.take_along_axis(positions, place_ids, axis=2)
    ghost_pos = jnp.where(is_live[:, None, :], ghost_pos, jnp.zeros_like(ghost_pos))
    near_x = jnp.concatenate([projected.reshape(CONFIGS, N_SPACE, ATOM_DEV, C), ghost_rows.reshape(CONFIGS, N_SPACE, GHOST, C)], axis=2).reshape(domain_count, near_count, C)
    own_pos = positions.reshape(CONFIGS, 3, N_SPACE, ATOM_DEV).transpose(0, 2, 1, 3)
    far_pos = ghost_pos.reshape(CONFIGS, 3, N_SPACE, GHOST).transpose(0, 2, 1, 3)
    near_pos = jnp.concatenate([own_pos, far_pos], axis=3).reshape(domain_count, 3, near_count)

    def domain_pass(pieces):
        own_h, own_place, near_rows, near_place, tile_block, species_ids, energy_cot = pieces
        mask = pair_weights(tile_block, ATOM_DEV, near_count)
        edge_table, moment_cot, energy, skip_term, gradients = rows_pass(own_h, own_place, mask, species_ids, energy_cot, near_rows, near_place, w_radial, w_mix, w_update, w_out, skip_gain)
        near_cot = lax.dot_general(edge_table.reshape(-1, near_count), moment_cot.reshape(-1, C), (((0,), (0,)), ((), ())), preferred_element_type=jnp.float32) * neighbour_scale
        return (energy, skip_term, near_cot, gradients)
    energy, skip_term, near_cot, gradients = lax.map(domain_pass, (features.reshape(domain_count, ATOM_DEV, C), own_pos.reshape(domain_count, 3, ATOM_DEV), near_x, near_pos, tile_mask.reshape(domain_count, TILES_OWN, TILES_NEAR), species.reshape(domain_count, ATOM_DEV), energy_grad.reshape(domain_count, ATOM_DEV)))
    near_cot = near_cot.reshape(CONFIGS, N_SPACE, near_count, C)
    own_cot = near_cot[:, :, :ATOM_DEV].reshape(CONFIGS, ATOMS, C)
    ghost_cot = near_cot[:, :, ATOM_DEV:].reshape(CONFIGS, N_SPACE * GHOST, C)
    ghost_cot = jnp.where(is_live[:, :, None], ghost_cot, jnp.zeros_like(ghost_cot))
    proj_cot = jax.vmap(lambda start_rows, target_ids, added_rows: start_rows.at[target_ids].add(added_rows))(own_cot, safe_ids, ghost_cot)
    proj_bf = proj_cot.astype(jnp.bfloat16).reshape(-1, C)
    flat_h = features.reshape(-1, C)
    feature_grad = lax.dot_general(proj_bf, w_proj, (((1,), (1,)), ((), ())), preferred_element_type=jnp.float32)
    feature_grad = (feature_grad + skip_term.reshape(-1, C)).reshape(CONFIGS, ATOMS, C)
    grad_scale = (CONFIGS * ATOMS) ** (-0.5)
    proj_grad = lax.dot_general(flat_h, proj_bf, (((0,), (0,)), ((), ())), preferred_element_type=jnp.float32) * grad_scale
    d_update, d_mix, d_radial, d_out, d_skip = [lax.optimization_barrier(jnp.sum(item, axis=0)) * grad_scale for item in gradients]
    energies = energy.reshape(CONFIGS, ATOMS)
    return (energies, feature_grad, proj_grad, d_radial, d_mix, d_update, d_out, d_skip)
```

```python
import functools
import math

import jax
import jax.numpy as jnp
from jax import lax
from jax.experimental import pallas as pl
from jax.experimental.pallas import tpu as pltpu
from jax.sharding import PartitionSpec as P

neighbour_scale = 0.0625
radial_step = 0.8
MESH = pl.DeviceIdType.MESH
HIGH = lax.Precision.HIGHEST
F32 = jnp.float32
BF16 = jnp.bfloat16


def loop(count, step):
    if count <= 16:
        for i in range(count):
            step(i)
    else:
        lax.fori_loop(0, count, lambda i, c: (step(i), c)[1], 0)


def edge_products(dx, dy, dz, weight, radial_count):
    xx, yy, zz = dx * dx, dy * dy, dz * dz
    r = jnp.sqrt(xx + yy + zz)
    radial = []
    for k in range(radial_count):
        t = r - radial_step * k if k else r
        radial.append(jnp.exp(-(t * t)) * weight)
    r3 = math.sqrt(3.0)
    shapes = [
        None,
        dx,
        dy,
        dz,
        r3 * dx * dy,
        r3 * dy * dz,
        0.5 * (2.0 * zz - xx - yy),
        r3 * dx * dz,
        0.5 * r3 * (xx - yy),
    ]
    return [b if y is None else y * b for y in shapes for b in radial]


def nt_dot(a, b, precision=None):
    return lax.dot_general(
        a, b, (((1,), (1,)), ((), ())), preferred_element_type=F32, precision=precision
    )


def tn_dot(a, b):
    return lax.dot_general(a, b, (((0,), (0,)), ((), ())), preferred_element_type=F32)


class Reduce:
    def __init__(self, refs, chunks, rows, stride, lin, total, parts):
        self.send, self.recv, self.back, self.s1, self.r1, self.s2, self.r2 = refs
        self.chunks, self.rows, self.stride = chunks, rows, stride
        self.lin, self.total, self.parts = lin, total, parts
        self.mine = lax.div(lin, stride)
        self.everyone = stride == 1 and chunks == total

    def peer(self, index):
        return {"space": lax.div(index, self.parts), "dp": lax.rem(index, self.parts)}

    def block(self, ref, chunk):
        return ref.at[pl.ds(pl.multiple_of(chunk * self.rows, self.rows), self.rows)]

    def owned(self, step):
        if self.everyone:
            step()
        else:
            pl.when((lax.rem(self.lin, self.stride) == 0) & (self.mine < self.chunks))(step)

    def unless_self(self, chunk, step):
        pl.when(chunk * self.stride != self.lin)(step)

    def out_copy(self, chunk):
        return pltpu.make_async_remote_copy(
            src_ref=self.block(self.send, chunk),
            dst_ref=self.recv.at[self.lin],
            send_sem=self.s1.at[chunk],
            recv_sem=self.r1.at[self.lin],
            device_id=self.peer(chunk * self.stride),
            device_id_type=MESH,
        )

    def in_copy(self, sender):
        return pltpu.make_async_remote_copy(
            src_ref=self.recv.at[sender],
            dst_ref=self.recv.at[sender],
            send_sem=self.s1.at[0],
            recv_sem=self.r1.at[sender],
            device_id=self.peer(sender),
            device_id_type=MESH,
        )

    def back_copy(self, target):
        return pltpu.make_async_remote_copy(
            src_ref=self.block(self.back, self.mine),
            dst_ref=self.block(self.back, self.mine),
            send_sem=self.s2.at[target],
            recv_sem=self.r2.at[self.mine],
            device_id=self.peer(target),
            device_id_type=MESH,
        )

    def home_copy(self, chunk):
        return pltpu.make_async_remote_copy(
            src_ref=self.block(self.back, chunk),
            dst_ref=self.block(self.back, chunk),
            send_sem=self.s2.at[0],
            recv_sem=self.r2.at[chunk],
            device_id=self.peer(chunk * self.stride),
            device_id_type=MESH,
        )

    def each_chunk(self, act):
        if self.everyone:
            loop(self.chunks - 1, lambda o: act(lax.rem(self.lin + 1 + o, self.chunks)))
        else:
            loop(self.chunks, lambda q: self.unless_self(q, lambda: act(q)))

    def each_peer(self, act):
        loop(self.total - 1, lambda o: act(lax.rem(self.lin + 1 + o, self.total)))

    def scatter(self):
        self.each_chunk(lambda q: self.out_copy(q).start())

    def collect(self, scale):
        def step():
            self.recv[self.lin] = self.block(self.send, self.mine)[...]
            self.each_peer(lambda t: self.in_copy(t).wait_recv())
            if self.total <= 16:
                acc = self.recv[0].astype(F32)
                for i in range(1, self.total):
                    acc = acc + self.recv[i].astype(F32)
            else:
                acc = lax.fori_loop(
                    1,
                    self.total,
                    lambda i, a: a + self.recv[i].astype(F32),
                    self.recv[0].astype(F32),
                )
            self.block(self.back, self.mine)[...] = (acc * scale).astype(self.back.dtype)
            self.each_peer(lambda t: self.back_copy(t).start())

        self.owned(step)

    def finish(self):
        self.each_chunk(lambda q: self.home_copy(q).wait_recv())

    def drain(self):
        self.each_chunk(lambda q: self.out_copy(q).wait_send())
        self.owned(lambda: self.each_peer(lambda t: self.back_copy(t).wait_send()))


def kernel(dims, *refs):
    spaces, parts, n, ghosts, channels, radial_count, species_count, tiles, scale = dims
    (
        feat_ref,
        pos_ref,
        spec_ref,
        ghost_ref,
        tile_ref,
        eg_ref,
        wproj_ref,
        wrad_ref,
        wmix_ref,
        wupd_ref,
        wout_ref,
        skip_ref,
        energy_ref,
        fgrad_ref,
        pgrad_ref,
        rgrad_ref,
        mgrad_ref,
        ugrad_ref,
        ograd_ref,
        sgrad_ref,
        table,
        turned,
        moments,
        density,
        near_x,
        small,
        near_pos,
        columns,
        near_columns,
        tile_pad,
        mask_rows,
        mask_cols,
        gain_pad,
        skip_row,
        mixed,
        cot_b,
        work,
        mcot,
        part_energy,
        turned_h,
        near_cot,
        nbr_x,
        nbr_small,
        ghost_in,
        u_send,
        u_recv,
        u_back,
        p_send,
        p_recv,
        p_back,
        s_send,
        s_recv,
        s_back,
        x_sem,
        u_s1,
        u_r1,
        u_s2,
        u_r2,
        p_s1,
        p_r1,
        p_s2,
        p_r2,
        s_s1,
        s_r1,
        s_s2,
        s_r2,
    ) = refs
    m = n + ghosts
    pk = 9 * radial_count
    total = spaces * parts
    me = lax.axis_index("space")
    lin = me * parts + lax.axis_index("dp")
    matrix_chunks = channels // 16
    matrix_stride = max(1, total // matrix_chunks)
    upd = Reduce(
        (u_send, u_recv, u_back, u_s1, u_r1, u_s2, u_r2),
        matrix_chunks, 16, matrix_stride, lin, total, parts,
    )
    prj = Reduce(
        (p_send, p_recv, p_back, p_s1, p_r1, p_s2, p_r2),
        matrix_chunks, 16, matrix_stride, lin, total, parts,
    )
    sml = Reduce(
        (s_send, s_recv, s_back, s_s1, s_r1, s_s2, s_r2), 3, 8, total // 4, lin, total, parts
    )

    @pl.when(me == 0)
    def _():
        nbr_x[0] = jnp.zeros((n, channels), BF16)
        nbr_small[0] = jnp.zeros((8, m), F32)
        ghost_in[0] = jnp.zeros((ghosts, channels), F32)

    @pl.when(me == spaces - 1)
    def _():
        nbr_x[1] = jnp.zeros((n, channels), BF16)
        nbr_small[1] = jnp.zeros((8, m), F32)
        ghost_in[1] = jnp.zeros((ghosts, channels), F32)

    barrier = pltpu.get_barrier_semaphore()
    upd.each_peer(
        lambda t: pl.semaphore_signal(
            barrier, inc=1, device_id=upd.peer(t), device_id_type=MESH
        )
    )

    small[...] = jnp.zeros((8, m), F32)
    small[0:3, 0:n] = pos_ref[0]
    small[3:4, 0:ghosts] = ghost_ref[0].astype(F32)
    small[4:5, 0:n] = eg_ref[...]
    small[5:6, 0:n] = spec_ref[...].astype(F32)
    own_h = feat_ref[0]
    near_x[0:n] = jnp.dot(own_h, wproj_ref[...], preferred_element_type=F32).astype(BF16)
    pl.semaphore_wait(barrier, total - 1)

    dp_at = lax.axis_index("dp")

    def exchange(ref, into, lane):
        pairs = []
        for side, target, there in ((0, me + 1, me < spaces - 1), (1, me - 1, me > 0)):
            source_there = me > 0 if side == 0 else me < spaces - 1
            copy = pltpu.make_async_remote_copy(
                src_ref=ref,
                dst_ref=into.at[side],
                send_sem=x_sem.at[lane, side],
                recv_sem=x_sem.at[lane + 1, side],
                device_id={"space": target, "dp": dp_at},
                device_id_type=MESH,
            )
            pairs.append((copy, there, source_there))
        return pairs

    def start(pairs):
        for copy, there, _ in pairs:
            pl.when(there)(copy.start)

    def arrive(pairs):
        for copy, _, source_there in pairs:
            pl.when(source_there)(copy.wait_recv)

    def sent(pairs):
        for copy, there, _ in pairs:
            pl.when(there)(copy.wait_send)

    rows_out = exchange(near_x.at[0:n], nbr_x, 0)
    small_out = exchange(small, nbr_small, 2)
    start(small_out)
    start(rows_out)

    tile_pad[...] = jnp.zeros(tile_pad.shape, F32)
    tile_pad[0 : tiles[0], 0 : tiles[1]] = tile_ref[0, 0].astype(F32)
    tile_size = n // tiles[0]
    flags = tile_pad[...]
    flags_turned = flags.T[0:8, :]
    at_m = lax.div(lax.broadcasted_iota(jnp.int32, (8, m), 1), tile_size)
    at_n = lax.div(lax.broadcasted_iota(jnp.int32, (8, n), 1), tile_size)
    by_row = jnp.zeros((8, m), F32)
    by_col = jnp.zeros((8, n), F32)
    for u in range(tiles[1]):
        by_row = jnp.where(at_m == u, flags[:, u : u + 1], by_row)
    for t in range(tiles[0]):
        by_col = jnp.where(at_n == t, flags_turned[:, t : t + 1], by_col)
    for t in range(8):
        mask_rows[t] = jnp.broadcast_to(by_row[t : t + 1], (8, m))
        mask_cols[t] = jnp.broadcast_to(by_col[t : t + 1], (8, n))
    columns[...] = small[...].T
    near_pos[...] = small[...]

    lanes = 128

    def fill_rows(block, chunks):
        at = pl.multiple_of(block * 16, 16)
        cols = columns[pl.ds(at, 16), :]
        ox, oy, oz = cols[:, 0:1], cols[:, 1:2], cols[:, 2:3]
        tile = lax.div(at, tile_size)
        for chunk in chunks:
            where = slice(chunk * lanes, (chunk + 1) * lanes)
            weight = jnp.broadcast_to(mask_rows[tile, 0:1, where], (16, lanes))
            if chunk * lanes < n:
                row = lax.broadcasted_iota(jnp.int32, (16, lanes), 0) + at
                col = lax.broadcasted_iota(jnp.int32, (16, lanes), 1) + chunk * lanes
                weight = jnp.where(row == col, 0.0, weight)
            dx = near_pos[0:1, where] - ox
            dy = near_pos[1:2, where] - oy
            dz = near_pos[2:3, where] - oz
            for i, v in enumerate(edge_products(dx, dy, dz, weight, radial_count)):
                table[i, pl.ds(at, 16), where] = v.astype(BF16)

    def fill_turned(block, own):
        at = pl.multiple_of(block * 16, 16)
        cols = columns[pl.ds(at, 16), :] if own else near_columns[pl.ds(at - n, 16), :]
        nx, ny, nz = cols[:, 0:1], cols[:, 1:2], cols[:, 2:3]
        tile = lax.div(at, tile_size)
        for chunk in range(n // lanes):
            where = slice(chunk * lanes, (chunk + 1) * lanes)
            weight = jnp.broadcast_to(mask_cols[tile, 0:1, where], (16, lanes))
            if own:
                row = lax.broadcasted_iota(jnp.int32, (16, lanes), 0) + at
                col = lax.broadcasted_iota(jnp.int32, (16, lanes), 1) + chunk * lanes
                weight = jnp.where(row == col, 0.0, weight)
            dx = nx - small[0:1, where]
            dy = ny - small[1:2, where]
            dz = nz - small[2:3, where]
            for i, v in enumerate(edge_products(dx, dy, dz, weight, radial_count)):
                to = slice(i * n + chunk * lanes, i * n + (chunk + 1) * lanes)
                turned[pl.ds(at, 16), to] = v.astype(BF16)

    own_chunks = range(n // lanes)
    far_chunks = range(n // lanes, m // lanes)

    @pl.loop(0, n // 16)
    def _(block):
        fill_rows(block, own_chunks)

    @pl.loop(0, n // 16)
    def _(block):
        fill_turned(block, True)

    turned_h[...] = own_h.T
    gain_pad[...] = jnp.zeros(gain_pad.shape, F32)
    gain_pad[0:species_count] = skip_ref[...]
    hot = (
        columns[0:n, 5:6] == lax.broadcasted_iota(jnp.int32, (n, 16), 1).astype(F32)
    ).astype(F32)
    skip_row[...] = jnp.dot(hot, gain_pad[...], precision=HIGH, preferred_element_type=F32)

    arrive(small_out)
    arrive(rows_out)
    base = (me * n).astype(F32)
    id_col = columns[0:ghosts, 3:4]
    id_row = small[3:4, 0:ghosts]
    live_col = jnp.where(id_col < 0.0, -1e6, id_col - base)
    live_row = jnp.where(id_row < 0.0, -1e6, id_row - base)
    at_lane = lax.broadcasted_iota(jnp.int32, (ghosts, n), 1).astype(F32)
    at_row = lax.broadcasted_iota(jnp.int32, (n, ghosts), 0).astype(F32)
    far_rows = jnp.zeros((ghosts, channels), F32)
    far_pos = jnp.zeros((8, ghosts), F32)
    for side, shift in ((0, float(n)), (1, -float(n))):
        pick = (live_col + shift == at_lane).astype(F32).astype(BF16)
        far_rows += jnp.dot(pick, nbr_x[side], preferred_element_type=F32)
        pick_row = (live_row + shift == at_row).astype(F32)
        far_pos += jnp.dot(
            nbr_small[side, :, 0:n], pick_row, precision=HIGH, preferred_element_type=F32
        )
    near_x[n:m] = far_rows.astype(BF16)
    near_pos[:, n:m] = far_pos
    near_columns[...] = far_pos.T

    @pl.loop(0, n // 16)
    def _(block):
        fill_rows(block, far_chunks)

    @pl.loop(0, 9)
    def _(p):
        at = p * radial_count
        lhs = table[pl.ds(at, radial_count)].reshape(radial_count * n, m)
        out = jnp.dot(lhs, near_x[...], preferred_element_type=F32) * neighbour_scale
        moments[pl.ds(at, radial_count)] = out.reshape(radial_count, n, channels)

    def halves():
        return [slice(h * lanes, (h + 1) * lanes) for h in range(channels // lanes)]

    def invariants_of(dens):
        return [
            dens[0],
            dens[0] * dens[0],
            dens[1] * dens[1] + dens[2] * dens[2] + dens[3] * dens[3],
            dens[4] * dens[4]
            + dens[5] * dens[5]
            + dens[6] * dens[6]
            + dens[7] * dens[7]
            + dens[8] * dens[8],
        ]

    @pl.loop(0, n // 16)
    def _(block):
        rows = pl.ds(pl.multiple_of(block * 16, 16), 16)
        for where in halves():
            weights = [wrad_ref[k : k + 1, where] for k in range(radial_count)]
            dens = []
            for p in range(9):
                acc = weights[0] * moments[p * radial_count, rows, where]
                for k in range(1, radial_count):
                    acc += weights[k] * moments[p * radial_count + k, rows, where]
                density[p, rows, where] = acc
                dens.append(acc)
            inv = invariants_of(dens)
            acc = wmix_ref[0:1, where] * inv[0]
            for q in range(1, 4):
                acc += wmix_ref[q : q + 1, where] * inv[q]
            mixed[rows, where] = acc.astype(BF16)

    work[...] = jnp.dot(mixed[...], wupd_ref[...], preferred_element_type=F32)

    def node_step(block, totals):
        rows = pl.ds(pl.multiple_of(block * 16, 16), 16)
        grad = columns[rows, 4:5]
        sums, energy = [], None
        for h, where in enumerate(halves()):
            own = feat_ref[0, rows, where].astype(F32)
            skip = skip_row[rows, where]
            update = work[rows, where] + own * skip
            readout = wout_ref[0:1, where].astype(F32)
            logistic = jax.nn.sigmoid(update)
            active = update * logistic
            share = active * readout
            energy = share if energy is None else energy + share
            cot = grad * readout * (logistic * (1.0 + update * (1.0 - logistic)))
            cot_b[rows, where] = cot.astype(BF16)
            fgrad_ref[0, rows, where] = cot * skip
            work[rows, where] = cot * own
            sums.append(totals[h] + grad * active)
        part_energy[rows, :] = energy
        return tuple(sums)

    zero = jnp.zeros((16, lanes), F32)
    out_sums = lax.fori_loop(
        0, n // 16, node_step, tuple(zero for _ in range(channels // lanes))
    )
    mcot[...] = nt_dot(cot_b[...], wupd_ref[...])
    u_send[...] = tn_dot(mixed[...], cot_b[...]).astype(BF16)
    upd.scatter()

    def grad_step(block, totals):
        rows = pl.ds(pl.multiple_of(block * 16, 16), 16)
        rad, mix = list(totals[0]), list(totals[1])
        for h, where in enumerate(halves()):
            dens = [density[p, rows, where] for p in range(9)]
            cot = mcot[rows, where]
            inv = invariants_of(dens)
            weighted = []
            for q in range(4):
                at = h * 4 + q
                mix[at] = mix[at] + cot * inv[q]
                weighted.append(wmix_ref[q : q + 1, where] * cot)
            w2, w3 = 2.0 * weighted[2], 2.0 * weighted[3]
            weights = [wrad_ref[k : k + 1, where] for k in range(radial_count)]
            for p in range(9):
                if p == 0:
                    dcot = weighted[0] + 2.0 * weighted[1] * dens[0]
                else:
                    dcot = (w2 if p < 4 else w3) * dens[p]
                for k in range(radial_count):
                    i = p * radial_count + k
                    at = h * radial_count + k
                    rad[at] = rad[at] + dcot * moments[i, rows, where]
                    table[i, rows, where] = (dcot * weights[k]).astype(BF16)
        return tuple(rad), tuple(mix)

    count = channels // lanes
    rad_sums, mix_sums = lax.fori_loop(
        0,
        n // 16,
        grad_step,
        (tuple(zero for _ in range(radial_count * count)), tuple(zero for _ in range(4 * count))),
    )

    hot_turned = (
        small[5:6, 0:n] == lax.broadcasted_iota(jnp.int32, (16, n), 0).astype(F32)
    ).astype(F32)
    s_send[...] = jnp.zeros(s_send.shape, F32)
    for h, where in enumerate(halves()):
        for k in range(radial_count):
            s_send[k : k + 1, where] = jnp.sum(
                rad_sums[h * radial_count + k], axis=0, keepdims=True
            )
        for q in range(4):
            s_send[4 + q : 5 + q, where] = jnp.sum(mix_sums[h * 4 + q], axis=0, keepdims=True)
        s_send[18:19, where] = jnp.sum(out_sums[h], axis=0, keepdims=True)
    s_send[8 : 8 + species_count] = jnp.dot(
        hot_turned, work[...], precision=HIGH, preferred_element_type=F32
    )[0:species_count]
    sml.scatter()

    @pl.loop(0, (m - n) // 16)
    def _(block):
        fill_turned(block + n // 16, False)

    step_pk = 6 if pk % 6 == 0 else 1

    def back_part(first, rows):
        near_cot[first : first + rows] = jnp.zeros((rows, channels), F32)

        @pl.loop(0, pk // step_pk)
        def _(j):
            lhs = turned[
                first : first + rows,
                pl.ds(pl.multiple_of(j * (step_pk * n), lanes), step_pk * n),
            ]
            rhs = table[pl.ds(j * step_pk, step_pk), :, 0:channels].reshape(
                step_pk * n, channels
            )
            near_cot[first : first + rows] += jnp.dot(lhs, rhs, preferred_element_type=F32)

        near_cot[first : first + rows] = near_cot[first : first + rows] * neighbour_scale

    back_part(n, ghosts)
    ghost_out = exchange(near_cot.at[n:m], ghost_in, 4)
    start(ghost_out)
    upd.collect(scale)
    back_part(0, n)
    sml.collect(scale)
    energy_ref[...] = jnp.sum(part_energy[...].T, axis=0, keepdims=True)

    arrive(ghost_out)
    returned = near_cot[0:n]
    for side in range(2):
        ids = nbr_small[side, 3:4, 0:ghosts] - base
        want = (ids == at_row).astype(F32)
        returned += jnp.dot(want, ghost_in[side], precision=HIGH, preferred_element_type=F32)
    proj_b = returned.astype(BF16)
    p_send[...] = jnp.dot(turned_h[...], proj_b, preferred_element_type=F32).astype(BF16)
    prj.scatter()
    fgrad_ref[0] = fgrad_ref[0] + nt_dot(proj_b, wproj_ref[...])
    prj.collect(scale)

    upd.finish()
    ugrad_ref[...] = u_back[...].astype(F32)
    sml.finish()
    rgrad_ref[...] = s_back[0:radial_count]
    mgrad_ref[...] = s_back[4:8]
    sgrad_ref[...] = s_back[8 : 8 + species_count]
    ograd_ref[...] = s_back[18:19]
    prj.finish()
    pgrad_ref[...] = p_back[...].astype(F32)

    sent(small_out)
    sent(rows_out)
    sent(ghost_out)
    upd.drain()
    sml.drain()
    prj.drain()


def body(spaces, parts, *args):
    features, positions, species, ghost_ids, tile_mask = args[:5]
    wout_at = 10
    args = list(args)
    args[wout_at] = args[wout_at].reshape(1, -1)
    _, n, channels = features.shape
    ghosts = ghost_ids.shape[-1]
    radial_count = args[7].shape[0]
    species_count = args[11].shape[0]
    tiles = tile_mask.shape[2:]
    m = n + ghosts
    pk = 9 * radial_count
    total = spaces * parts
    scale = (spaces * parts * n * features.shape[0]) ** (-0.5)
    chunks = channels // 16
    vmem = pltpu.VMEM
    dma = pltpu.SemaphoreType.DMA
    dims = (spaces, parts, n, ghosts, channels, radial_count, species_count, tiles, scale)
    scratch = [
        vmem((pk, n, m), BF16),
        vmem((m, pk * n), BF16),
        vmem((pk, n, channels), F32),
        vmem((9, n, channels), F32),
        vmem((m, channels), BF16),
        vmem((8, m), F32),
        vmem((8, m), F32),
        vmem((m, 8), F32),
        vmem((ghosts, 8), F32),
        vmem((8, 128), F32),
        vmem((8, 8, m), F32),
        vmem((8, 8, n), F32),
        vmem((16, channels), F32),
        vmem((n, channels), F32),
        vmem((n, channels), BF16),
        vmem((n, channels), BF16),
        vmem((n, channels), F32),
        vmem((n, channels), F32),
        vmem((n, 128), F32),
        vmem((channels, n), BF16),
        vmem((m, channels), F32),
        vmem((2, n, channels), BF16),
        vmem((2, 8, m), F32),
        vmem((2, ghosts, channels), F32),
    ]
    for _ in range(2):
        scratch += [
            vmem((channels, channels), BF16),
            vmem((total, 16, channels), BF16),
            vmem((channels, channels), BF16),
        ]
    scratch += [vmem((24, channels), F32), vmem((total, 8, channels), F32), vmem((24, channels), F32)]
    scratch += [dma((6, 2))]
    for _ in range(2):
        scratch += [dma((chunks,)), dma((total,)), dma((total,)), dma((chunks,))]
    scratch += [dma((3,)), dma((total,)), dma((total,)), dma((3,))]
    whole = pl.BlockSpec(memory_space=pltpu.VMEM)
    shapes = [
        (1, n),
        (1, n, channels),
        (channels, channels),
        (radial_count, channels),
        (4, channels),
        (channels, channels),
        (1, channels),
        (species_count, channels),
    ]
    outs = pl.pallas_call(
        functools.partial(kernel, dims),
        out_shape=[jax.ShapeDtypeStruct(s, F32) for s in shapes],
        in_specs=[whole] * len(args),
        out_specs=[whole] * len(shapes),
        scratch_shapes=scratch,
        compiler_params=pltpu.CompilerParams(
            collective_id=0, has_side_effects=True, vmem_limit_bytes=60 * 1024 * 1024
        ),
    )(*args)
    outs = list(outs)
    outs[6] = outs[6].reshape(channels)
    return tuple(outs)


def solution(mesh):
    in_specs = (
        P(("groups", "dp"), "space", None),
        P(("groups", "dp"), None, "space"),
        P(("groups", "dp"), "space"),
        P(("groups", "dp"), "space", None),
        P(("groups", "dp"), "space", None, None),
        P(("groups", "dp"), "space"),
        P(),
        P(),
        P(),
        P(),
        P(),
        P(),
    )
    out_specs = (
        P(("groups", "dp"), "space"),
        P(("groups", "dp"), "space", None),
        P("groups", None),
        P("groups", None),
        P("groups", None),
        P("groups", None),
        P("groups"),
        P("groups", None),
    )
    step = functools.partial(body, mesh.shape["space"], mesh.shape["dp"])
    return jax.shard_map(step, mesh=mesh, in_specs=in_specs, out_specs=out_specs, check_vma=False)
```

```python
import functools
import math

import jax
import jax.numpy as jnp
from jax import lax
from jax.experimental import pallas as pl
from jax.experimental.pallas import tpu as pltpu
from jax.sharding import PartitionSpec as P

neighbour_scale = 0.0625
radial_step = 0.8
MESH = pl.DeviceIdType.MESH
HIGH = lax.Precision.HIGHEST
F32 = jnp.float32
BF16 = jnp.bfloat16


def loop(count, step):
    if count <= 16:
        for i in range(count):
            step(i)
    else:
        lax.fori_loop(0, count, lambda i, c: (step(i), c)[1], 0)


def edge_products(dx, dy, dz, weight, radial_count):
    xx, yy, zz = dx * dx, dy * dy, dz * dz
    r = jnp.sqrt(xx + yy + zz)
    radial = []
    for k in range(radial_count):
        t = r - radial_step * k if k else r
        radial.append(jnp.exp(-(t * t)) * weight)
    r3 = math.sqrt(3.0)
    shapes = [
        None,
        dx,
        dy,
        dz,
        r3 * dx * dy,
        r3 * dy * dz,
        0.5 * (2.0 * zz - xx - yy),
        r3 * dx * dz,
        0.5 * r3 * (xx - yy),
    ]
    return [b if y is None else y * b for y in shapes for b in radial]


def nt_dot(a, b, precision=None):
    return lax.dot_general(
        a, b, (((1,), (1,)), ((), ())), preferred_element_type=F32, precision=precision
    )


def tn_dot(a, b):
    return lax.dot_general(a, b, (((0,), (0,)), ((), ())), preferred_element_type=F32)


class Reduce:
    def __init__(self, refs, chunks, rows, stride, lin, total, parts):
        self.send, self.recv, self.back, self.s1, self.r1, self.s2, self.r2 = refs
        self.chunks, self.rows, self.stride = chunks, rows, stride
        self.lin, self.total, self.parts = lin, total, parts
        self.mine = lax.div(lin, stride)
        self.everyone = stride == 1 and chunks == total

    def peer(self, index):
        return {"space": lax.div(index, self.parts), "dp": lax.rem(index, self.parts)}

    def block(self, ref, chunk):
        return ref.at[pl.ds(pl.multiple_of(chunk * self.rows, self.rows), self.rows)]

    def owned(self, step):
        if self.everyone:
            step()
        else:
            pl.when((lax.rem(self.lin, self.stride) == 0) & (self.mine < self.chunks))(step)

    def unless_self(self, chunk, step):
        pl.when(chunk * self.stride != self.lin)(step)

    def out_copy(self, chunk):
        return pltpu.make_async_remote_copy(
            src_ref=self.block(self.send, chunk),
            dst_ref=self.recv.at[self.lin],
            send_sem=self.s1.at[chunk],
            recv_sem=self.r1.at[self.lin],
            device_id=self.peer(chunk * self.stride),
            device_id_type=MESH,
        )

    def in_copy(self, sender):
        return pltpu.make_async_remote_copy(
            src_ref=self.recv.at[sender],
            dst_ref=self.recv.at[sender],
            send_sem=self.s1.at[0],
            recv_sem=self.r1.at[sender],
            device_id=self.peer(sender),
            device_id_type=MESH,
        )

    def back_copy(self, target):
        return pltpu.make_async_remote_copy(
            src_ref=self.block(self.back, self.mine),
            dst_ref=self.block(self.back, self.mine),
            send_sem=self.s2.at[target],
            recv_sem=self.r2.at[self.mine],
            device_id=self.peer(target),
            device_id_type=MESH,
        )

    def home_copy(self, chunk):
        return pltpu.make_async_remote_copy(
            src_ref=self.block(self.back, chunk),
            dst_ref=self.block(self.back, chunk),
            send_sem=self.s2.at[0],
            recv_sem=self.r2.at[chunk],
            device_id=self.peer(chunk * self.stride),
            device_id_type=MESH,
        )

    def each_chunk(self, act):
        if self.everyone:
            loop(self.chunks - 1, lambda o: act(lax.rem(self.lin + 1 + o, self.chunks)))
        else:
            loop(self.chunks, lambda q: self.unless_self(q, lambda: act(q)))

    def each_peer(self, act):
        loop(self.total - 1, lambda o: act(lax.rem(self.lin + 1 + o, self.total)))

    def scatter(self):
        self.each_chunk(lambda q: self.out_copy(q).start())

    def collect(self, scale):
        def step():
            self.recv[self.lin] = self.block(self.send, self.mine)[...]
            self.each_peer(lambda t: self.in_copy(t).wait_recv())
            if self.total <= 16:
                acc = self.recv[0].astype(F32)
                for i in range(1, self.total):
                    acc = acc + self.recv[i].astype(F32)
            else:
                acc = lax.fori_loop(
                    1,
                    self.total,
                    lambda i, a: a + self.recv[i].astype(F32),
                    self.recv[0].astype(F32),
                )
            self.block(self.back, self.mine)[...] = (acc * scale).astype(self.back.dtype)
            self.each_peer(lambda t: self.back_copy(t).start())

        self.owned(step)

    def finish(self):
        self.each_chunk(lambda q: self.home_copy(q).wait_recv())

    def drain(self):
        self.each_chunk(lambda q: self.out_copy(q).wait_send())
        self.owned(lambda: self.each_peer(lambda t: self.back_copy(t).wait_send()))


def kernel(dims, *refs):
    spaces, parts, n, ghosts, channels, radial_count, species_count, tiles, scale = dims
    (
        feat_ref,
        pos_ref,
        spec_ref,
        ghost_ref,
        tile_ref,
        eg_ref,
        wproj_ref,
        wrad_ref,
        wmix_ref,
        wupd_ref,
        wout_ref,
        skip_ref,
        energy_ref,
        fgrad_ref,
        pgrad_ref,
        rgrad_ref,
        mgrad_ref,
        ugrad_ref,
        ograd_ref,
        sgrad_ref,
        table,
        turned,
        moments,
        density,
        near_x,
        small,
        near_pos,
        columns,
        near_columns,
        tile_pad,
        mask_rows,
        mask_cols,
        gain_pad,
        skip_row,
        mixed,
        cot_b,
        work,
        mcot,
        part_energy,
        turned_h,
        near_cot,
        nbr_x,
        sent_x,
        sent_cot,
        wout_row,
        nbr_small,
        ghost_in,
        u_send,
        u_recv,
        u_back,
        p_send,
        p_recv,
        p_back,
        s_send,
        s_recv,
        s_back,
        x_sem,
        u_s1,
        u_r1,
        u_s2,
        u_r2,
        p_s1,
        p_r1,
        p_s2,
        p_r2,
        s_s1,
        s_r1,
        s_s2,
        s_r2,
    ) = refs
    m = n + ghosts
    pk = 9 * radial_count
    total = spaces * parts
    me = lax.axis_index("space")
    lin = me * parts + lax.axis_index("dp")
    matrix_chunks = channels // 16
    matrix_stride = max(1, total // matrix_chunks)
    upd = Reduce(
        (u_send, u_recv, u_back, u_s1, u_r1, u_s2, u_r2),
        matrix_chunks, 16, matrix_stride, lin, total, parts,
    )
    prj = Reduce(
        (p_send, p_recv, p_back, p_s1, p_r1, p_s2, p_r2),
        matrix_chunks, 16, matrix_stride, lin, total, parts,
    )
    sml = Reduce(
        (s_send, s_recv, s_back, s_s1, s_r1, s_s2, s_r2), 3, 8, total // 4, lin, total, parts
    )

    @pl.when(me == 0)
    def _():
        nbr_x[0] = jnp.zeros((ghosts, channels), BF16)
        nbr_small[0] = jnp.zeros((8, m), F32)
        ghost_in[0] = jnp.zeros((ghosts, channels), BF16)

    @pl.when(me == spaces - 1)
    def _():
        nbr_x[1] = jnp.zeros((ghosts, channels), BF16)
        nbr_small[1] = jnp.zeros((8, m), F32)
        ghost_in[1] = jnp.zeros((ghosts, channels), BF16)

    barrier = pltpu.get_barrier_semaphore()
    upd.each_peer(
        lambda t: pl.semaphore_signal(
            barrier, inc=1, device_id=upd.peer(t), device_id_type=MESH
        )
    )

    wout_row[...] = jnp.broadcast_to(wout_ref[...].astype(F32)[None, :], (8, channels))
    small[...] = jnp.zeros((8, m), F32)
    for axis in range(3):
        small[axis : axis + 1, 0:n] = pos_ref[axis]
    small[3:4, 0:ghosts] = ghost_ref[0].astype(F32)
    small[4:5, 0:n] = eg_ref[...]
    small[5:6, 0:n] = spec_ref[...].astype(F32)
    own_h = feat_ref[0]
    near_x[0:n] = jnp.dot(own_h, wproj_ref[...], preferred_element_type=F32).astype(BF16)
    pl.semaphore_wait(barrier, total - 1)

    dp_at = lax.axis_index("dp")

    def exchange(sources, into, lane):
        pairs = []
        for side, target, there in ((0, me + 1, me < spaces - 1), (1, me - 1, me > 0)):
            ref = sources[1 - side]
            source_there = me > 0 if side == 0 else me < spaces - 1
            copy = pltpu.make_async_remote_copy(
                src_ref=ref,
                dst_ref=into.at[side],
                send_sem=x_sem.at[lane, side],
                recv_sem=x_sem.at[lane + 1, side],
                device_id={"space": target, "dp": dp_at},
                device_id_type=MESH,
            )
            pairs.append((copy, there, source_there))
        return pairs

    def start(pairs):
        for copy, there, _ in pairs:
            pl.when(there)(copy.start)

    def arrive(pairs):
        for copy, _, source_there in pairs:
            pl.when(source_there)(copy.wait_recv)

    def sent(pairs):
        for copy, there, _ in pairs:
            pl.when(there)(copy.wait_send)

    small_out = exchange((small, small), nbr_small, 2)
    start(small_out)

    tile_pad[...] = jnp.zeros(tile_pad.shape, F32)
    for t in range(tiles[0]):
        tile_pad[t : t + 1, 0 : tiles[1]] = tile_ref[t].astype(F32)
    tile_size = n // tiles[0]
    flags = tile_pad[...]
    flags_turned = flags.T[0:8, :]
    at_m = lax.div(lax.broadcasted_iota(jnp.int32, (8, m), 1), tile_size)
    at_n = lax.div(lax.broadcasted_iota(jnp.int32, (8, n), 1), tile_size)
    by_row = jnp.zeros((8, m), F32)
    by_col = jnp.zeros((8, n), F32)
    for u in range(tiles[1]):
        by_row = jnp.where(at_m == u, flags[:, u : u + 1], by_row)
    for t in range(tiles[0]):
        by_col = jnp.where(at_n == t, flags_turned[:, t : t + 1], by_col)
    for t in range(8):
        mask_rows[t] = jnp.broadcast_to(by_row[t : t + 1], (8, m))
        mask_cols[t] = jnp.broadcast_to(by_col[t : t + 1], (8, n))
    columns[...] = small[...].T
    near_pos[...] = small[...]

    lanes = 128

    def fill_rows(block, chunks):
        at = pl.multiple_of(block * 16, 16)
        cols = columns[pl.ds(at, 16), :]
        ox, oy, oz = cols[:, 0:1], cols[:, 1:2], cols[:, 2:3]
        tile = lax.div(at, tile_size)
        for chunk in chunks:
            where = slice(chunk * lanes, (chunk + 1) * lanes)
            weight = jnp.broadcast_to(mask_rows[tile, 0:1, where], (16, lanes))
            if chunk * lanes < n:
                row = lax.broadcasted_iota(jnp.int32, (16, lanes), 0) + at
                col = lax.broadcasted_iota(jnp.int32, (16, lanes), 1) + chunk * lanes
                weight = jnp.where(row == col, 0.0, weight)
            dx = near_pos[0:1, where] - ox
            dy = near_pos[1:2, where] - oy
            dz = near_pos[2:3, where] - oz
            for i, v in enumerate(edge_products(dx, dy, dz, weight, radial_count)):
                table[i, pl.ds(at, 16), where] = v.astype(BF16)

    def fill_turned(block, own):
        at = pl.multiple_of(block * 16, 16)
        cols = columns[pl.ds(at, 16), :] if own else near_columns[pl.ds(at - n, 16), :]
        nx, ny, nz = cols[:, 0:1], cols[:, 1:2], cols[:, 2:3]
        tile = lax.div(at, tile_size)
        for chunk in range(n // lanes):
            where = slice(chunk * lanes, (chunk + 1) * lanes)
            weight = jnp.broadcast_to(mask_cols[tile, 0:1, where], (16, lanes))
            if own:
                row = lax.broadcasted_iota(jnp.int32, (16, lanes), 0) + at
                col = lax.broadcasted_iota(jnp.int32, (16, lanes), 1) + chunk * lanes
                weight = jnp.where(row == col, 0.0, weight)
            dx = nx - small[0:1, where]
            dy = ny - small[1:2, where]
            dz = nz - small[2:3, where]
            for i, v in enumerate(edge_products(dx, dy, dz, weight, radial_count)):
                to = slice(i * n + chunk * lanes, i * n + (chunk + 1) * lanes)
                turned[pl.ds(at, 16), to] = v.astype(BF16)

    own_chunks = range(n // lanes)
    far_chunks = range(n // lanes, m // lanes)

    @pl.loop(0, n // 16)
    def _(block):
        fill_rows(block, own_chunks)

    arrive(small_out)
    base = (me * n).astype(F32)
    at_lane = lax.broadcasted_iota(jnp.int32, (ghosts, n), 1).astype(F32)
    at_row = lax.broadcasted_iota(jnp.int32, (n, ghosts), 0).astype(F32)
    for side in range(2):
        asked = nbr_small[side, :, 0:ghosts].T[:, 3:4] - base
        pick = (asked == at_lane).astype(F32).astype(BF16)
        picked = jnp.dot(pick, near_x[0:n], preferred_element_type=F32)
        sent_x[side] = picked.astype(BF16)
    rows_out = exchange((sent_x.at[0], sent_x.at[1]), nbr_x, 0)
    start(rows_out)

    @pl.loop(0, n // 16)
    def _(block):
        fill_turned(block, True)

    turned_h[...] = own_h.T
    gain_pad[...] = jnp.zeros(gain_pad.shape, F32)
    gain_pad[0:species_count] = skip_ref[...]
    hot = (
        columns[0:n, 5:6] == lax.broadcasted_iota(jnp.int32, (n, 16), 1).astype(F32)
    ).astype(F32)
    skip_row[...] = jnp.dot(hot, gain_pad[...], precision=HIGH, preferred_element_type=F32)

    id_row = small[3:4, 0:ghosts]
    live_row = jnp.where(id_row < 0.0, -1e6, id_row - base)
    terms, picks = [], []
    for side, shift in ((0, float(n)), (1, -float(n))):
        rest = nbr_small[side, :, 0:n]
        high = rest.astype(BF16).astype(F32)
        rest = rest - high
        middle = rest.astype(BF16).astype(F32)
        low = rest - middle
        terms.append(jnp.concatenate([high, middle, low, jnp.zeros_like(low)], axis=0))
        picks.append((live_row + shift == at_row).astype(F32).astype(BF16))
    split = jnp.dot(
        jnp.concatenate(terms, axis=1).astype(BF16),
        jnp.concatenate(picks, axis=0),
        preferred_element_type=F32,
    )
    far_pos = (split[0:8] + split[8:16]) + split[16:24]
    near_pos[:, n:m] = far_pos
    near_columns[...] = far_pos.T
    arrive(rows_out)
    near_x[n:m] = (nbr_x[0].astype(F32) + nbr_x[1].astype(F32)).astype(BF16)

    @pl.loop(0, n // 16)
    def _(block):
        fill_rows(block, far_chunks)

    @pl.loop(0, 9)
    def _(p):
        at = p * radial_count
        lhs = table[pl.ds(at, radial_count)].reshape(radial_count * n, m)
        out = jnp.dot(lhs, near_x[...], preferred_element_type=F32)
        moments[pl.ds(at, radial_count)] = out.reshape(radial_count, n, channels)

    def halves():
        return [slice(h * lanes, (h + 1) * lanes) for h in range(channels // lanes)]

    def invariants_of(dens):
        return [
            dens[0],
            dens[0] * dens[0],
            dens[1] * dens[1] + dens[2] * dens[2] + dens[3] * dens[3],
            dens[4] * dens[4]
            + dens[5] * dens[5]
            + dens[6] * dens[6]
            + dens[7] * dens[7]
            + dens[8] * dens[8],
        ]

    @pl.loop(0, n // 16)
    def _(block):
        rows = pl.ds(pl.multiple_of(block * 16, 16), 16)
        for where in halves():
            weights = [
                wrad_ref[k : k + 1, where] * neighbour_scale for k in range(radial_count)
            ]
            dens = []
            for p in range(9):
                acc = weights[0] * moments[p * radial_count, rows, where]
                for k in range(1, radial_count):
                    acc += weights[k] * moments[p * radial_count + k, rows, where]
                density[p, rows, where] = acc
                dens.append(acc)
            inv = invariants_of(dens)
            acc = wmix_ref[0:1, where] * inv[0]
            for q in range(1, 4):
                acc += wmix_ref[q : q + 1, where] * inv[q]
            mixed[rows, where] = acc.astype(BF16)

    work[...] = jnp.dot(mixed[...], wupd_ref[...], preferred_element_type=F32)

    node_rows = math.gcd(n, 64)

    def node_step(block, totals):
        rows = pl.ds(pl.multiple_of(block * node_rows, node_rows), node_rows)
        grad = columns[rows, 4:5]
        sums, energy = [], None
        for h, where in enumerate(halves()):
            own = feat_ref[0, rows, where].astype(F32)
            skip = skip_row[rows, where]
            update = work[rows, where] + own * skip
            readout = wout_row[0:1, where]
            logistic = jax.nn.sigmoid(update)
            active = update * logistic
            share = active * readout
            energy = share if energy is None else energy + share
            cot = grad * readout * (logistic * (1.0 + update * (1.0 - logistic)))
            cot_b[rows, where] = cot.astype(BF16)
            fgrad_ref[0, rows, where] = cot * skip
            work[rows, where] = cot * own
            sums.append(totals[h] + grad * active)
        part_energy[rows, :] = energy
        return tuple(sums)

    zero = jnp.zeros((node_rows, lanes), F32)
    out_sums = lax.fori_loop(
        0, n // node_rows, node_step, tuple(zero for _ in range(channels // lanes))
    )
    mcot[...] = nt_dot(cot_b[...], wupd_ref[...])
    u_send[...] = tn_dot(mixed[...], cot_b[...]).astype(BF16)
    upd.scatter()

    def grad_step(block, totals):
        rows = pl.ds(pl.multiple_of(block * 16, 16), 16)
        rad, mix = list(totals[0]), list(totals[1])
        for h, where in enumerate(halves()):
            dens = [density[p, rows, where] for p in range(9)]
            cot = mcot[rows, where]
            inv = invariants_of(dens)
            weighted = []
            for q in range(4):
                at = h * 4 + q
                mix[at] = mix[at] + cot * inv[q]
                weighted.append(wmix_ref[q : q + 1, where] * cot)
            w2, w3 = 2.0 * weighted[2], 2.0 * weighted[3]
            weights = [wrad_ref[k : k + 1, where] for k in range(radial_count)]
            for p in range(9):
                if p == 0:
                    dcot = weighted[0] + 2.0 * weighted[1] * dens[0]
                else:
                    dcot = (w2 if p < 4 else w3) * dens[p]
                for k in range(radial_count):
                    i = p * radial_count + k
                    at = h * radial_count + k
                    rad[at] = rad[at] + dcot * moments[i, rows, where]
                    table[i, rows, where] = (dcot * weights[k]).astype(BF16)
        return tuple(rad), tuple(mix)

    count = channels // lanes
    zero = jnp.zeros((16, lanes), F32)
    rad_sums, mix_sums = lax.fori_loop(
        0,
        n // 16,
        grad_step,
        (tuple(zero for _ in range(radial_count * count)), tuple(zero for _ in range(4 * count))),
    )

    hot_turned = (
        small[5:6, 0:n] == lax.broadcasted_iota(jnp.int32, (16, n), 0).astype(F32)
    ).astype(F32)
    s_send[...] = jnp.zeros(s_send.shape, F32)
    for h, where in enumerate(halves()):
        for k in range(radial_count):
            s_send[k : k + 1, where] = neighbour_scale * jnp.sum(
                rad_sums[h * radial_count + k], axis=0, keepdims=True
            )
        for q in range(4):
            s_send[4 + q : 5 + q, where] = jnp.sum(mix_sums[h * 4 + q], axis=0, keepdims=True)
        s_send[18:19, where] = jnp.sum(out_sums[h], axis=0, keepdims=True)
    s_send[8 : 8 + species_count] = jnp.dot(
        hot_turned, work[...], precision=HIGH, preferred_element_type=F32
    )[0:species_count]
    sml.scatter()

    @pl.loop(0, (m - n) // 16)
    def _(block):
        fill_turned(block + n // 16, False)

    step_pk = 6 if pk % 6 == 0 else 1

    def back_part(first, rows):
        near_cot[first : first + rows] = jnp.zeros((rows, channels), F32)

        @pl.loop(0, pk // step_pk)
        def _(j):
            lhs = turned[
                first : first + rows,
                pl.ds(pl.multiple_of(j * (step_pk * n), lanes), step_pk * n),
            ]
            rhs = table[pl.ds(j * step_pk, step_pk), :, 0:channels].reshape(
                step_pk * n, channels
            )
            near_cot[first : first + rows] += jnp.dot(lhs, rhs, preferred_element_type=F32)


    back_part(n, ghosts)
    sent_cot[...] = (near_cot[n:m] * neighbour_scale).astype(BF16)
    ghost_out = exchange((sent_cot, sent_cot), ghost_in, 4)
    start(ghost_out)
    upd.collect(scale)
    back_part(0, n)
    sml.collect(scale)
    energy_ref[...] = jnp.sum(part_energy[...].T, axis=0, keepdims=True)

    arrive(ghost_out)
    wants = [
        (nbr_small[side, 3:4, 0:ghosts] - base == at_row).astype(F32).astype(BF16)
        for side in range(2)
    ]
    returned = near_cot[0:n] * neighbour_scale + jnp.dot(
        jnp.concatenate(wants, axis=1),
        ghost_in[...].reshape(2 * ghosts, channels),
        preferred_element_type=F32,
    )
    proj_b = returned.astype(BF16)
    p_send[...] = jnp.dot(turned_h[...], proj_b, preferred_element_type=F32).astype(BF16)
    prj.scatter()
    fgrad_ref[0] = fgrad_ref[0] + nt_dot(proj_b, wproj_ref[...])
    prj.collect(scale)

    upd.finish()
    ugrad_ref[...] = u_back[...].astype(F32)
    sml.finish()
    rgrad_ref[...] = s_back[0:radial_count]
    mgrad_ref[...] = s_back[4:8]
    sgrad_ref[...] = s_back[8 : 8 + species_count]
    ograd_ref[...] = s_back[18:19]
    prj.finish()
    pgrad_ref[...] = p_back[...].astype(F32)

    sent(small_out)
    sent(rows_out)
    sent(ghost_out)
    upd.drain()
    sml.drain()
    prj.drain()


def hand_over(*refs):
    count = len(refs) // 2
    sems = refs[-1]
    copies = [
        pltpu.make_async_copy(refs[i], refs[count + i], sems.at[i]) for i in range(count)
    ]
    for copy in copies:
        copy.start()
    for copy in copies:
        copy.wait()


def body(spaces, parts, *args):
    features, positions, species, ghost_ids, tile_mask = args[:5]
    args = list(args)
    _, n, channels = features.shape
    args[1] = positions.reshape(3, 1, n)
    args[4] = tile_mask.reshape(tile_mask.shape[2], 1, tile_mask.shape[3])
    ghosts = ghost_ids.shape[-1]
    radial_count = args[7].shape[0]
    species_count = args[11].shape[0]
    tiles = tile_mask.shape[2:]
    m = n + ghosts
    pk = 9 * radial_count
    total = spaces * parts
    scale = (spaces * parts * n * features.shape[0]) ** (-0.5)
    chunks = channels // 16
    vmem = pltpu.VMEM
    dma = pltpu.SemaphoreType.DMA
    dims = (spaces, parts, n, ghosts, channels, radial_count, species_count, tiles, scale)
    scratch = [
        vmem((pk, n, m), BF16),
        vmem((m, pk * n), BF16),
        vmem((pk, n, channels), F32),
        vmem((9, n, channels), F32),
        vmem((m, channels), BF16),
        vmem((8, m), F32),
        vmem((8, m), F32),
        vmem((m, 8), F32),
        vmem((ghosts, 8), F32),
        vmem((8, 128), F32),
        vmem((8, 8, m), F32),
        vmem((8, 8, n), F32),
        vmem((16, channels), F32),
        vmem((n, channels), F32),
        vmem((n, channels), BF16),
        vmem((n, channels), BF16),
        vmem((n, channels), F32),
        vmem((n, channels), F32),
        vmem((n, 128), F32),
        vmem((channels, n), BF16),
        vmem((m, channels), F32),
        vmem((2, ghosts, channels), BF16),
        vmem((2, ghosts, channels), BF16),
        vmem((ghosts, channels), BF16),
        vmem((8, channels), F32),
        vmem((2, 8, m), F32),
        vmem((2, ghosts, channels), BF16),
    ]
    for _ in range(2):
        scratch += [
            vmem((channels, channels), BF16),
            vmem((total, 16, channels), BF16),
            vmem((channels, channels), BF16),
        ]
    scratch += [vmem((24, channels), F32), vmem((total, 8, channels), F32), vmem((24, channels), F32)]
    scratch += [dma((6, 2))]
    for _ in range(2):
        scratch += [dma((chunks,)), dma((total,)), dma((total,)), dma((chunks,))]
    scratch += [dma((3,)), dma((total,)), dma((total,)), dma((3,))]
    whole = pl.BlockSpec(memory_space=pltpu.VMEM)
    shapes = [
        (1, n),
        (1, n, channels),
        (channels, channels),
        (radial_count, channels),
        (4, channels),
        (channels, channels),
        (1, channels),
        (species_count, channels),
    ]
    outs = pl.pallas_call(
        functools.partial(kernel, dims),
        out_shape=[jax.ShapeDtypeStruct(s, F32) for s in shapes],
        in_specs=[whole] * len(args),
        out_specs=[whole] * len(shapes),
        scratch_shapes=scratch,
        compiler_params=pltpu.CompilerParams(
            collective_id=0, has_side_effects=True, vmem_limit_bytes=60 * 1024 * 1024
        ),
    )(*args)
    outs = pl.pallas_call(
        hand_over,
        out_shape=[jax.ShapeDtypeStruct(s, F32) for s in shapes],
        in_specs=[pl.BlockSpec(memory_space=pl.ANY)] * len(shapes),
        out_specs=[pl.BlockSpec(memory_space=pl.ANY)] * len(shapes),
        scratch_shapes=[dma((len(shapes),))],
    )(*outs)
    outs = list(outs)
    outs[6] = outs[6].reshape(channels)
    return tuple(outs)


def solution(mesh):
    in_specs = (
        P(("groups", "dp"), "space", None),
        P(("groups", "dp"), None, "space"),
        P(("groups", "dp"), "space"),
        P(("groups", "dp"), "space", None),
        P(("groups", "dp"), "space", None, None),
        P(("groups", "dp"), "space"),
        P(),
        P(),
        P(),
        P(),
        P(),
        P(),
    )
    out_specs = (
        P(("groups", "dp"), "space"),
        P(("groups", "dp"), "space", None),
        P("groups", None),
        P("groups", None),
        P("groups", None),
        P("groups", None),
        P("groups"),
        P("groups", None),
    )
    step = functools.partial(body, mesh.shape["space"], mesh.shape["dp"])
    return jax.shard_map(step, mesh=mesh, in_specs=in_specs, out_specs=out_specs, check_vma=False)
```

```python
import functools
import math

import jax
import jax.numpy as jnp
from jax import lax
from jax.experimental import pallas as pl
from jax.experimental.pallas import tpu as pltpu
from jax.sharding import PartitionSpec as P

neighbour_scale = 0.0625
radial_step = 0.8
MESH = pl.DeviceIdType.MESH
HIGH = lax.Precision.HIGHEST
F32 = jnp.float32
BF16 = jnp.bfloat16


def loop(count, step):
    if count <= 16:
        for i in range(count):
            step(i)
    else:
        lax.fori_loop(0, count, lambda i, c: (step(i), c)[1], 0)


def edge_products(dx, dy, dz, weight, radial_count):
    xx, yy, zz = dx * dx, dy * dy, dz * dz
    r = jnp.sqrt(xx + yy + zz)
    radial = []
    for k in range(radial_count):
        t = r - radial_step * k if k else r
        radial.append(jnp.exp(-(t * t)) * weight)
    r3 = math.sqrt(3.0)
    shapes = [
        None,
        dx,
        dy,
        dz,
        r3 * dx * dy,
        r3 * dy * dz,
        0.5 * (2.0 * zz - xx - yy),
        r3 * dx * dz,
        0.5 * r3 * (xx - yy),
    ]
    return [b if y is None else y * b for y in shapes for b in radial]


def nt_dot(a, b, precision=None):
    return lax.dot_general(
        a, b, (((1,), (1,)), ((), ())), preferred_element_type=F32, precision=precision
    )


def tn_dot(a, b):
    return lax.dot_general(a, b, (((0,), (0,)), ((), ())), preferred_element_type=F32)


class Reduce:
    def __init__(self, refs, chunks, rows, stride, lin, total, parts):
        self.send, self.recv, self.back, self.s1, self.r1, self.s2, self.r2 = refs
        self.chunks, self.rows, self.stride = chunks, rows, stride
        self.lin, self.total, self.parts = lin, total, parts
        self.mine = lax.div(lin, stride)
        self.everyone = stride == 1 and chunks == total

    def peer(self, index):
        return {"space": lax.div(index, self.parts), "dp": lax.rem(index, self.parts)}

    def block(self, ref, chunk):
        return ref.at[pl.ds(pl.multiple_of(chunk * self.rows, self.rows), self.rows)]

    def owned(self, step):
        if self.everyone:
            step()
        else:
            pl.when((lax.rem(self.lin, self.stride) == 0) & (self.mine < self.chunks))(step)

    def unless_self(self, chunk, step):
        pl.when(chunk * self.stride != self.lin)(step)

    def out_copy(self, chunk):
        return pltpu.make_async_remote_copy(
            src_ref=self.block(self.send, chunk),
            dst_ref=self.recv.at[self.lin],
            send_sem=self.s1.at[chunk],
            recv_sem=self.r1.at[self.lin],
            device_id=self.peer(chunk * self.stride),
            device_id_type=MESH,
        )

    def in_copy(self, sender):
        return pltpu.make_async_remote_copy(
            src_ref=self.recv.at[sender],
            dst_ref=self.recv.at[sender],
            send_sem=self.s1.at[0],
            recv_sem=self.r1.at[sender],
            device_id=self.peer(sender),
            device_id_type=MESH,
        )

    def back_copy(self, target):
        return pltpu.make_async_remote_copy(
            src_ref=self.block(self.back, self.mine),
            dst_ref=self.block(self.back, self.mine),
            send_sem=self.s2.at[target],
            recv_sem=self.r2.at[self.mine],
            device_id=self.peer(target),
            device_id_type=MESH,
        )

    def home_copy(self, chunk):
        return pltpu.make_async_remote_copy(
            src_ref=self.block(self.back, chunk),
            dst_ref=self.block(self.back, chunk),
            send_sem=self.s2.at[0],
            recv_sem=self.r2.at[chunk],
            device_id=self.peer(chunk * self.stride),
            device_id_type=MESH,
        )

    def each_chunk(self, act):
        if self.everyone:
            loop(self.chunks - 1, lambda o: act(lax.rem(self.lin + 1 + o, self.chunks)))
        else:
            loop(self.chunks, lambda q: self.unless_self(q, lambda: act(q)))

    def each_peer(self, act):
        loop(self.total - 1, lambda o: act(lax.rem(self.lin + 1 + o, self.total)))

    def scatter(self):
        self.each_chunk(lambda q: self.out_copy(q).start())

    def collect(self, scale):
        def step():
            self.recv[self.lin] = self.block(self.send, self.mine)[...]
            self.each_peer(lambda t: self.in_copy(t).wait_recv())
            if self.total <= 16:
                acc = self.recv[0].astype(F32)
                for i in range(1, self.total):
                    acc = acc + self.recv[i].astype(F32)
            else:
                acc = lax.fori_loop(
                    1,
                    self.total,
                    lambda i, a: a + self.recv[i].astype(F32),
                    self.recv[0].astype(F32),
                )
            self.block(self.back, self.mine)[...] = (acc * scale).astype(self.back.dtype)
            self.each_peer(lambda t: self.back_copy(t).start())

        self.owned(step)

    def finish(self):
        self.each_chunk(lambda q: self.home_copy(q).wait_recv())

    def drain(self):
        self.each_chunk(lambda q: self.out_copy(q).wait_send())
        self.owned(lambda: self.each_peer(lambda t: self.back_copy(t).wait_send()))


def kernel(dims, *refs):
    spaces, parts, n, ghosts, channels, radial_count, species_count, tiles, scale = dims
    (
        feat_ref,
        pos_ref,
        spec_ref,
        ghost_ref,
        tile_ref,
        eg_ref,
        wproj_ref,
        wrad_ref,
        wmix_ref,
        wupd_ref,
        wout_ref,
        skip_ref,
        energy_ref,
        fgrad_ref,
        pgrad_ref,
        rgrad_ref,
        mgrad_ref,
        ugrad_ref,
        ograd_ref,
        sgrad_ref,
        table,
        turned,
        moments,
        density,
        near_x,
        small,
        near_pos,
        columns,
        near_columns,
        tile_pad,
        mask_rows,
        mask_cols,
        gain_pad,
        skip_row,
        mixed,
        cot_b,
        work,
        mcot,
        part_energy,
        turned_h,
        near_cot,
        nbr_x,
        sent_x,
        sent_cot,
        wout_row,
        nbr_small,
        ghost_in,
        u_send,
        u_recv,
        u_back,
        p_send,
        p_recv,
        p_back,
        s_send,
        s_recv,
        s_back,
        x_sem,
        u_s1,
        u_r1,
        u_s2,
        u_r2,
        p_s1,
        p_r1,
        p_s2,
        p_r2,
        s_s1,
        s_r1,
        s_s2,
        s_r2,
    ) = refs
    m = n + ghosts
    pk = 9 * radial_count
    total = spaces * parts
    me = lax.axis_index("space")
    lin = me * parts + lax.axis_index("dp")
    matrix_chunks = channels // 16
    matrix_stride = max(1, total // matrix_chunks)
    upd = Reduce(
        (u_send, u_recv, u_back, u_s1, u_r1, u_s2, u_r2),
        matrix_chunks, 16, matrix_stride, lin, total, parts,
    )
    prj = Reduce(
        (p_send, p_recv, p_back, p_s1, p_r1, p_s2, p_r2),
        matrix_chunks, 16, matrix_stride, lin, total, parts,
    )
    sml = Reduce(
        (s_send, s_recv, s_back, s_s1, s_r1, s_s2, s_r2), 3, 8, total // 4, lin, total, parts
    )

    @pl.when(me == 0)
    def _():
        nbr_x[0] = jnp.zeros((ghosts, channels), BF16)
        nbr_small[0] = jnp.zeros((8, m), F32)
        ghost_in[0] = jnp.zeros((ghosts, channels), BF16)

    @pl.when(me == spaces - 1)
    def _():
        nbr_x[1] = jnp.zeros((ghosts, channels), BF16)
        nbr_small[1] = jnp.zeros((8, m), F32)
        ghost_in[1] = jnp.zeros((ghosts, channels), BF16)

    barrier = pltpu.get_barrier_semaphore()
    upd.each_peer(
        lambda t: pl.semaphore_signal(
            barrier, inc=1, device_id=upd.peer(t), device_id_type=MESH
        )
    )

    wout_row[...] = jnp.broadcast_to(wout_ref[...].astype(F32)[None, :], (8, channels))
    small[...] = jnp.zeros((8, m), F32)
    for axis in range(3):
        small[axis : axis + 1, 0:n] = pos_ref[axis]
    small[3:4, 0:ghosts] = ghost_ref[0].astype(F32)
    small[4:5, 0:n] = eg_ref[...]
    small[5:6, 0:n] = spec_ref[...].astype(F32)
    own_h = feat_ref[0]
    near_x[0:n] = jnp.dot(own_h, wproj_ref[...], preferred_element_type=F32).astype(BF16)
    pl.semaphore_wait(barrier, total - 1)

    dp_at = lax.axis_index("dp")

    def exchange(sources, into, lane):
        pairs = []
        for side, target, there in ((0, me + 1, me < spaces - 1), (1, me - 1, me > 0)):
            ref = sources[1 - side]
            source_there = me > 0 if side == 0 else me < spaces - 1
            copy = pltpu.make_async_remote_copy(
                src_ref=ref,
                dst_ref=into.at[side],
                send_sem=x_sem.at[lane, side],
                recv_sem=x_sem.at[lane + 1, side],
                device_id={"space": target, "dp": dp_at},
                device_id_type=MESH,
            )
            pairs.append((copy, there, source_there))
        return pairs

    def start(pairs):
        for copy, there, _ in pairs:
            pl.when(there)(copy.start)

    def arrive(pairs):
        for copy, _, source_there in pairs:
            pl.when(source_there)(copy.wait_recv)

    def sent(pairs):
        for copy, there, _ in pairs:
            pl.when(there)(copy.wait_send)

    small_out = exchange((small, small), nbr_small, 2)
    start(small_out)

    tile_pad[...] = jnp.zeros(tile_pad.shape, F32)
    for t in range(tiles[0]):
        tile_pad[t : t + 1, 0 : tiles[1]] = tile_ref[t].astype(F32)
    tile_size = n // tiles[0]
    flags = tile_pad[...]
    flags_turned = flags.T[0:8, :]
    at_m = lax.div(lax.broadcasted_iota(jnp.int32, (8, m), 1), tile_size)
    at_n = lax.div(lax.broadcasted_iota(jnp.int32, (8, n), 1), tile_size)
    by_row = jnp.zeros((8, m), F32)
    by_col = jnp.zeros((8, n), F32)
    for u in range(tiles[1]):
        by_row = jnp.where(at_m == u, flags[:, u : u + 1], by_row)
    for t in range(tiles[0]):
        by_col = jnp.where(at_n == t, flags_turned[:, t : t + 1], by_col)
    for t in range(8):
        mask_rows[t] = jnp.broadcast_to(by_row[t : t + 1], (8, m))
        mask_cols[t] = jnp.broadcast_to(by_col[t : t + 1], (8, n))
    columns[...] = small[...].T
    near_pos[...] = small[...]

    lanes = 128

    def fill_rows(block, chunks):
        at = pl.multiple_of(block * 16, 16)
        cols = columns[pl.ds(at, 16), :]
        ox, oy, oz = cols[:, 0:1], cols[:, 1:2], cols[:, 2:3]
        tile = lax.div(at, tile_size)
        for chunk in chunks:
            where = slice(chunk * lanes, (chunk + 1) * lanes)
            weight = jnp.broadcast_to(mask_rows[tile, 0:1, where], (16, lanes))
            if chunk * lanes < n:
                row = lax.broadcasted_iota(jnp.int32, (16, lanes), 0) + at
                col = lax.broadcasted_iota(jnp.int32, (16, lanes), 1) + chunk * lanes
                weight = jnp.where(row == col, 0.0, weight)
            dx = near_pos[0:1, where] - ox
            dy = near_pos[1:2, where] - oy
            dz = near_pos[2:3, where] - oz
            for i, v in enumerate(edge_products(dx, dy, dz, weight, radial_count)):
                table[i, pl.ds(at, 16), where] = v.astype(BF16)

    def fill_turned(block, own):
        at = pl.multiple_of(block * 16, 16)
        cols = columns[pl.ds(at, 16), :] if own else near_columns[pl.ds(at - n, 16), :]
        nx, ny, nz = cols[:, 0:1], cols[:, 1:2], cols[:, 2:3]
        tile = lax.div(at, tile_size)
        for chunk in range(n // lanes):
            where = slice(chunk * lanes, (chunk + 1) * lanes)
            weight = jnp.broadcast_to(mask_cols[tile, 0:1, where], (16, lanes))
            if own:
                row = lax.broadcasted_iota(jnp.int32, (16, lanes), 0) + at
                col = lax.broadcasted_iota(jnp.int32, (16, lanes), 1) + chunk * lanes
                weight = jnp.where(row == col, 0.0, weight)
            dx = nx - small[0:1, where]
            dy = ny - small[1:2, where]
            dz = nz - small[2:3, where]
            for i, v in enumerate(edge_products(dx, dy, dz, weight, radial_count)):
                to = slice(i * n + chunk * lanes, i * n + (chunk + 1) * lanes)
                turned[pl.ds(at, 16), to] = v.astype(BF16)

    own_chunks = range(n // lanes)
    far_chunks = range(n // lanes, m // lanes)

    @pl.loop(0, n // 16)
    def _(block):
        fill_rows(block, own_chunks)

    arrive(small_out)
    base = (me * n).astype(F32)
    at_lane = lax.broadcasted_iota(jnp.int32, (ghosts, n), 1).astype(F32)
    at_row = lax.broadcasted_iota(jnp.int32, (n, ghosts), 0).astype(F32)
    for side in range(2):
        asked = nbr_small[side, :, 0:ghosts].T[:, 3:4] - base
        pick = (asked == at_lane).astype(F32).astype(BF16)
        picked = jnp.dot(pick, near_x[0:n], preferred_element_type=F32)
        sent_x[side] = picked.astype(BF16)
    rows_out = exchange((sent_x.at[0], sent_x.at[1]), nbr_x, 0)
    start(rows_out)

    @pl.loop(0, n // 16)
    def _(block):
        fill_turned(block, True)

    turned_h[...] = own_h.T
    gain_pad[...] = jnp.zeros(gain_pad.shape, F32)
    gain_pad[0:species_count] = skip_ref[...]
    hot = (
        columns[0:n, 5:6] == lax.broadcasted_iota(jnp.int32, (n, 16), 1).astype(F32)
    ).astype(F32)
    skip_row[...] = jnp.dot(hot, gain_pad[...], precision=HIGH, preferred_element_type=F32)

    id_row = small[3:4, 0:ghosts]
    live_row = jnp.where(id_row < 0.0, -1e6, id_row - base)
    terms, picks = [], []
    for side, shift in ((0, float(n)), (1, -float(n))):
        rest = nbr_small[side, :, 0:n]
        high = rest.astype(BF16).astype(F32)
        rest = rest - high
        middle = rest.astype(BF16).astype(F32)
        low = rest - middle
        terms.append(jnp.concatenate([high, middle, low, jnp.zeros_like(low)], axis=0))
        picks.append((live_row + shift == at_row).astype(F32).astype(BF16))
    split = jnp.dot(
        jnp.concatenate(terms, axis=1).astype(BF16),
        jnp.concatenate(picks, axis=0),
        preferred_element_type=F32,
    )
    far_pos = (split[0:8] + split[8:16]) + split[16:24]
    near_pos[:, n:m] = far_pos
    near_columns[...] = far_pos.T
    arrive(rows_out)
    near_x[n:m] = (nbr_x[0].astype(F32) + nbr_x[1].astype(F32)).astype(BF16)

    @pl.loop(0, n // 16)
    def _(block):
        fill_rows(block, far_chunks)

    @pl.loop(0, 9)
    def _(p):
        at = p * radial_count
        lhs = table[pl.ds(at, radial_count)].reshape(radial_count * n, m)
        out = jnp.dot(lhs, near_x[...], preferred_element_type=F32)
        moments[pl.ds(at, radial_count)] = out.reshape(radial_count, n, channels)

    def halves():
        return [slice(h * lanes, (h + 1) * lanes) for h in range(channels // lanes)]

    def invariants_of(dens):
        return [
            dens[0],
            dens[0] * dens[0],
            dens[1] * dens[1] + dens[2] * dens[2] + dens[3] * dens[3],
            dens[4] * dens[4]
            + dens[5] * dens[5]
            + dens[6] * dens[6]
            + dens[7] * dens[7]
            + dens[8] * dens[8],
        ]

    @pl.loop(0, n // 16)
    def _(block):
        rows = pl.ds(pl.multiple_of(block * 16, 16), 16)
        for where in halves():
            weights = [
                wrad_ref[k : k + 1, where] * neighbour_scale for k in range(radial_count)
            ]
            dens = []
            for p in range(9):
                acc = weights[0] * moments[p * radial_count, rows, where]
                for k in range(1, radial_count):
                    acc += weights[k] * moments[p * radial_count + k, rows, where]
                density[p, rows, where] = acc
                dens.append(acc)
            inv = invariants_of(dens)
            acc = wmix_ref[0:1, where] * inv[0]
            for q in range(1, 4):
                acc += wmix_ref[q : q + 1, where] * inv[q]
            mixed[rows, where] = acc.astype(BF16)

    work[...] = jnp.dot(mixed[...], wupd_ref[...], preferred_element_type=F32)

    node_rows = math.gcd(n, 64)

    def node_step(block, totals):
        rows = pl.ds(pl.multiple_of(block * node_rows, node_rows), node_rows)
        grad = columns[rows, 4:5]
        sums, energy = [], None
        for h, where in enumerate(halves()):
            own = feat_ref[0, rows, where].astype(F32)
            skip = skip_row[rows, where]
            update = work[rows, where] + own * skip
            readout = wout_row[0:1, where]
            logistic = jax.nn.sigmoid(update)
            active = update * logistic
            share = active * readout
            energy = share if energy is None else energy + share
            cot = grad * readout * (logistic * (1.0 + update * (1.0 - logistic)))
            cot_b[rows, where] = cot.astype(BF16)
            fgrad_ref[0, rows, where] = cot * skip
            work[rows, where] = cot * own
            sums.append(totals[h] + grad * active)
        part_energy[rows, :] = energy
        return tuple(sums)

    zero = jnp.zeros((node_rows, lanes), F32)
    out_sums = lax.fori_loop(
        0, n // node_rows, node_step, tuple(zero for _ in range(channels // lanes))
    )
    mcot[...] = nt_dot(cot_b[...], wupd_ref[...])
    u_send[...] = tn_dot(mixed[...], cot_b[...]).astype(BF16)
    upd.scatter()

    def grad_step(block, totals):
        rows = pl.ds(pl.multiple_of(block * 16, 16), 16)
        rad, mix = list(totals[0]), list(totals[1])
        for h, where in enumerate(halves()):
            dens = [density[p, rows, where] for p in range(9)]
            cot = mcot[rows, where]
            inv = invariants_of(dens)
            weighted = []
            for q in range(4):
                at = h * 4 + q
                mix[at] = mix[at] + cot * inv[q]
                weighted.append(wmix_ref[q : q + 1, where] * cot)
            w2, w3 = 2.0 * weighted[2], 2.0 * weighted[3]
            weights = [wrad_ref[k : k + 1, where] for k in range(radial_count)]
            for p in range(9):
                if p == 0:
                    dcot = weighted[0] + 2.0 * weighted[1] * dens[0]
                else:
                    dcot = (w2 if p < 4 else w3) * dens[p]
                for k in range(radial_count):
                    i = p * radial_count + k
                    at = h * radial_count + k
                    rad[at] = rad[at] + dcot * moments[i, rows, where]
                    table[i, rows, where] = (dcot * weights[k]).astype(BF16)
        return tuple(rad), tuple(mix)

    count = channels // lanes
    zero = jnp.zeros((16, lanes), F32)
    rad_sums, mix_sums = lax.fori_loop(
        0,
        n // 16,
        grad_step,
        (tuple(zero for _ in range(radial_count * count)), tuple(zero for _ in range(4 * count))),
    )

    hot_turned = (
        small[5:6, 0:n] == lax.broadcasted_iota(jnp.int32, (16, n), 0).astype(F32)
    ).astype(F32)
    s_send[...] = jnp.zeros(s_send.shape, F32)
    for h, where in enumerate(halves()):
        for k in range(radial_count):
            s_send[k : k + 1, where] = neighbour_scale * jnp.sum(
                rad_sums[h * radial_count + k], axis=0, keepdims=True
            )
        for q in range(4):
            s_send[4 + q : 5 + q, where] = jnp.sum(mix_sums[h * 4 + q], axis=0, keepdims=True)
        s_send[18:19, where] = jnp.sum(out_sums[h], axis=0, keepdims=True)
    s_send[8 : 8 + species_count] = jnp.dot(
        hot_turned, work[...], precision=HIGH, preferred_element_type=F32
    )[0:species_count]
    sml.scatter()

    @pl.loop(0, (m - n) // 16)
    def _(block):
        fill_turned(block + n // 16, False)

    step_pk = 6 if pk % 6 == 0 else 1

    def back_part(first, rows):
        near_cot[first : first + rows] = jnp.zeros((rows, channels), F32)

        @pl.loop(0, pk // step_pk)
        def _(j):
            lhs = turned[
                first : first + rows,
                pl.ds(pl.multiple_of(j * (step_pk * n), lanes), step_pk * n),
            ]
            rhs = table[pl.ds(j * step_pk, step_pk), :, 0:channels].reshape(
                step_pk * n, channels
            )
            near_cot[first : first + rows] += jnp.dot(lhs, rhs, preferred_element_type=F32)


    back_part(n, ghosts)
    sent_cot[...] = (near_cot[n:m] * neighbour_scale).astype(BF16)
    ghost_out = exchange((sent_cot, sent_cot), ghost_in, 4)
    start(ghost_out)
    upd.collect(scale)
    back_part(0, n)
    sml.collect(scale)
    energy_ref[...] = jnp.sum(part_energy[...].T, axis=0, keepdims=True)

    arrive(ghost_out)
    wants = [
        (nbr_small[side, 3:4, 0:ghosts] - base == at_row).astype(F32).astype(BF16)
        for side in range(2)
    ]
    returned = near_cot[0:n] * neighbour_scale + jnp.dot(
        jnp.concatenate(wants, axis=1),
        ghost_in[...].reshape(2 * ghosts, channels),
        preferred_element_type=F32,
    )
    proj_b = returned.astype(BF16)
    p_send[...] = jnp.dot(turned_h[...], proj_b, preferred_element_type=F32).astype(BF16)
    prj.scatter()
    fgrad_ref[0] = fgrad_ref[0] + nt_dot(proj_b, wproj_ref[...])
    prj.collect(scale)

    upd.finish()
    ugrad_ref[...] = u_back[...].astype(F32)
    sml.finish()
    rgrad_ref[...] = s_back[0:radial_count]
    mgrad_ref[...] = s_back[4:8]
    sgrad_ref[...] = s_back[8 : 8 + species_count]
    ograd_ref[...] = s_back[18:19]
    prj.finish()
    pgrad_ref[...] = p_back[...].astype(F32)

    sent(small_out)
    sent(rows_out)
    sent(ghost_out)
    upd.drain()
    sml.drain()
    prj.drain()


def hand_over(*refs):
    count = len(refs) // 2
    for source, target in zip(refs[:count], refs[count:]):
        target[...] = source[...]


def body(spaces, parts, *args):
    features, positions, species, ghost_ids, tile_mask = args[:5]
    args = list(args)
    _, n, channels = features.shape
    args[1] = positions.reshape(3, 1, n)
    args[4] = tile_mask.reshape(tile_mask.shape[2], 1, tile_mask.shape[3])
    ghosts = ghost_ids.shape[-1]
    radial_count = args[7].shape[0]
    species_count = args[11].shape[0]
    tiles = tile_mask.shape[2:]
    m = n + ghosts
    pk = 9 * radial_count
    total = spaces * parts
    scale = (spaces * parts * n * features.shape[0]) ** (-0.5)
    chunks = channels // 16
    vmem = pltpu.VMEM
    dma = pltpu.SemaphoreType.DMA
    dims = (spaces, parts, n, ghosts, channels, radial_count, species_count, tiles, scale)
    scratch = [
        vmem((pk, n, m), BF16),
        vmem((m, pk * n), BF16),
        vmem((pk, n, channels), F32),
        vmem((9, n, channels), F32),
        vmem((m, channels), BF16),
        vmem((8, m), F32),
        vmem((8, m), F32),
        vmem((m, 8), F32),
        vmem((ghosts, 8), F32),
        vmem((8, 128), F32),
        vmem((8, 8, m), F32),
        vmem((8, 8, n), F32),
        vmem((16, channels), F32),
        vmem((n, channels), F32),
        vmem((n, channels), BF16),
        vmem((n, channels), BF16),
        vmem((n, channels), F32),
        vmem((n, channels), F32),
        vmem((n, 128), F32),
        vmem((channels, n), BF16),
        vmem((m, channels), F32),
        vmem((2, ghosts, channels), BF16),
        vmem((2, ghosts, channels), BF16),
        vmem((ghosts, channels), BF16),
        vmem((8, channels), F32),
        vmem((2, 8, m), F32),
        vmem((2, ghosts, channels), BF16),
    ]
    for _ in range(2):
        scratch += [
            vmem((channels, channels), BF16),
            vmem((total, 16, channels), BF16),
            vmem((channels, channels), BF16),
        ]
    scratch += [vmem((24, channels), F32), vmem((total, 8, channels), F32), vmem((24, channels), F32)]
    scratch += [dma((6, 2))]
    for _ in range(2):
        scratch += [dma((chunks,)), dma((total,)), dma((total,)), dma((chunks,))]
    scratch += [dma((3,)), dma((total,)), dma((total,)), dma((3,))]
    whole = pl.BlockSpec(memory_space=pltpu.VMEM)
    shapes = [
        (1, n),
        (1, n, channels),
        (channels, channels),
        (radial_count, channels),
        (4, channels),
        (channels, channels),
        (1, channels),
        (species_count, channels),
    ]
    outs = pl.pallas_call(
        functools.partial(kernel, dims),
        out_shape=[jax.ShapeDtypeStruct(s, F32) for s in shapes],
        in_specs=[whole] * len(args),
        out_specs=[whole] * len(shapes),
        scratch_shapes=scratch,
        compiler_params=pltpu.CompilerParams(
            collective_id=0, has_side_effects=True, vmem_limit_bytes=60 * 1024 * 1024
        ),
    )(*args)
    outs = pl.pallas_call(
        hand_over,
        out_shape=[jax.ShapeDtypeStruct(s, F32) for s in shapes],
        in_specs=[whole] * len(shapes),
        out_specs=[whole] * len(shapes),
    )(*outs)
    outs = list(outs)
    outs[6] = outs[6].reshape(channels)
    return tuple(outs)


def solution(mesh):
    in_specs = (
        P(("groups", "dp"), "space", None),
        P(("groups", "dp"), None, "space"),
        P(("groups", "dp"), "space"),
        P(("groups", "dp"), "space", None),
        P(("groups", "dp"), "space", None, None),
        P(("groups", "dp"), "space"),
        P(),
        P(),
        P(),
        P(),
        P(),
        P(),
    )
    out_specs = (
        P(("groups", "dp"), "space"),
        P(("groups", "dp"), "space", None),
        P("groups", None),
        P("groups", None),
        P("groups", None),
        P("groups", None),
        P("groups"),
        P("groups", None),
    )
    step = functools.partial(body, mesh.shape["space"], mesh.shape["dp"])
    return jax.shard_map(step, mesh=mesh, in_specs=in_specs, out_specs=out_specs, check_vma=False)
```
